32 devices in a mesh: section: 4 (over z), ctx: 8 (over y, x, core).
Axes of the slice: x: 2, y: 2, z: 4, core: 2. Of those that a mesh axis runs over, the one named last changes fastest.
Arguments:
- query_rows: bfloat16 [4, 2048, 2048], P('section', 'ctx'), may hold values from -40 to 40
- key_rows: bfloat16 [4, 2048, 1024], P('section', 'ctx'), may hold values from -6 to 6
- value_rows: bfloat16 [4, 2048, 1024], P('section', 'ctx'), may hold values from -6 to 6
- finished_grad: bfloat16 [4, 2048, 2048], P('section', 'ctx'), may hold values from -96 to 96
- doc_lengths: int32 [4], replicated, may hold values from 1 to 1024, as said below
Outputs:
- query_grad: bfloat16 [4, 2048, 2048], P('section', 'ctx')
- key_grad: bfloat16 [4, 2048, 1024], P('section', 'ctx')
- value_grad: bfloat16 [4, 2048, 1024], P('section', 'ctx')
The draws below stay inside these ranges and needn't reach their ends.
Inputs may be any that keep to these rules, and one draw needn't show every extreme that they name: `doc_lengths`: document lengths add up to 2048; the longest is exactly 1024.
All inputs are finite; a program needn't handle non-finite values.
Results may differ from the reference program's by a relative error of at most 0.04.
Values may be sent and summed in bfloat16 or wider, within the bound.
A program may use at most 128 MiB of HBM per device.

```python
import jax
import jax.numpy as jnp
from jax import lax

ROWS = 256
WINDOW = 1024
HEADS = 16
KV_HEADS = 8
HEAD_DIM = 128
GROUP = 2
SECTIONS = 4
SEQ = 2048
MOST_DOC = 1024


def draw_key_rows(key, part):
    drawn = jax.random.truncated_normal(jax.random.fold_in(key, 101), -6.0, 6.0, (SECTIONS, SEQ, KV_HEADS * HEAD_DIM), jnp.float32)
    return drawn.astype(jnp.bfloat16)


def draw_query_rows(key, part):
    drawn = jax.random.truncated_normal(jax.random.fold_in(key, 201), -6.0, 6.0, (SECTIONS, SEQ, HEADS * HEAD_DIM), jnp.float32)
    return drawn.astype(jnp.bfloat16)


def draw_doc_lengths(key, part):
    remain = SEQ - MOST_DOC
    first_most = max(1, remain - WINDOW)
    first_len = jax.random.randint(jax.random.fold_in(key, 301), (), 1, first_most + 1).astype(jnp.int32)
    rest = (remain - first_len).astype(jnp.int32)
    third_len = jax.random.randint(jax.random.fold_in(key, 302), (), 1, rest).astype(jnp.int32)
    fourth_len = (rest - third_len).astype(jnp.int32)
    return jnp.stack([first_len, jnp.int32(MOST_DOC), third_len, fourth_len]).astype(jnp.int32)


def block_levels(own_key, dims, pieces, low, largest):
    gain = 1.0
    for dim, parts in pieces:
        heights = jax.random.uniform(jax.random.fold_in(jax.random.fold_in(own_key, 6), dim), (parts,), jnp.float32, low / len(pieces), largest / len(pieces))
        gain = gain * jnp.repeat(jnp.exp(heights), dims[dim] // parts).reshape((-1,) + (1,) * (len(dims) - 1 - dim))
    return gain


def scatter_about(own_key, shape, deviation, reach, cuts=(), kind=jnp.bfloat16):
    factor_of = block_levels(own_key, shape, cuts, -0.22, 0.18) if cuts else 1.0
    result = jax.random.normal(own_key, shape, jnp.float32) * deviation * factor_of
    return jnp.minimum(jnp.maximum(result, -reach), reach).astype(kind)


def setup_inputs(seed: int = 0) -> dict:
    arg_keys = jax.random.split(jax.random.key(seed), 6)
    query_rows = draw_query_rows(jax.random.fold_in(arg_keys[5], 71), 0)
    key_rows = draw_key_rows(jax.random.fold_in(arg_keys[5], 71), 0)
    value_rows = scatter_about(arg_keys[2], (SECTIONS, SEQ, KV_HEADS * HEAD_DIM), 1.0, 6.0, ((0, 4), (1, 8)))
    finished_grad = scatter_about(arg_keys[3], (SECTIONS, SEQ, HEADS * HEAD_DIM), 16.0, 96.0, ((0, 4), (1, 8)))
    doc_lengths = draw_doc_lengths(jax.random.fold_in(arg_keys[5], 71), 0)
    return dict(query_rows=query_rows, key_rows=key_rows, value_rows=value_rows, finished_grad=finished_grad, doc_lengths=doc_lengths)


SCORE_SCALE = 168.0 ** -0.5


def doc_number(positions, doc_lengths):
    ends = jnp.cumsum(doc_lengths).astype(jnp.int32)
    return jnp.sum((positions[:, None] >= ends[None, :]).astype(jnp.int32), axis=1).astype(jnp.int32)


def window_mask(query_pos, key_pos, doc_lengths):
    same_doc = doc_number(query_pos, doc_lengths)[:, None] == doc_number(key_pos, doc_lengths)[None, :]
    spacing = query_pos[:, None] - key_pos[None, :]
    return same_doc & (spacing >= 0) & (spacing < WINDOW) & (key_pos[None, :] >= 0)


def to_half(values):
    return lax.optimization_barrier(values.astype(jnp.bfloat16)).astype(jnp.float32)


def split_round(block_term):
    return jnp.concatenate([to_half(block_term[:WINDOW]), block_term[WINDOW:]], axis=0)


def section_grads(queries, keys_in, values_in, arriving, doc_lengths):
    span = WINDOW + ROWS
    width = keys_in.shape[1]
    padded_keys = jnp.concatenate([jnp.zeros((WINDOW, width), keys_in.dtype), keys_in], axis=0)
    padded_values = jnp.concatenate([jnp.zeros((WINDOW, width), values_in.dtype), values_in], axis=0)

    def step(carry, block):
        acc_keys, acc_values = carry
        start = (block * ROWS).astype(jnp.int32)
        query_block = lax.dynamic_slice_in_dim(queries, start, ROWS, 0).astype(jnp.float32).reshape(ROWS, KV_HEADS, GROUP, HEAD_DIM)
        grad_block = lax.dynamic_slice_in_dim(arriving, start, ROWS, 0).astype(jnp.float32).reshape(ROWS, KV_HEADS, GROUP, HEAD_DIM)
        key_block = lax.dynamic_slice_in_dim(padded_keys, start, span, 0).astype(jnp.float32).reshape(span, KV_HEADS, HEAD_DIM)
        value_block = lax.dynamic_slice_in_dim(padded_values, start, span, 0).astype(jnp.float32).reshape(span, KV_HEADS, HEAD_DIM)
        query_pos = start + jnp.arange(ROWS, dtype=jnp.int32)
        key_pos = start - WINDOW + jnp.arange(span, dtype=jnp.int32)
        allowed = window_mask(query_pos, key_pos, doc_lengths)
        scores = SCORE_SCALE * jnp.einsum('rhjd,khd->hjrk', query_block, key_block)
        scores = jnp.where(allowed[None, None], scores, -jnp.inf)
        highest = jnp.max(scores, axis=-1, keepdims=True)
        log_total = highest + jnp.log(jnp.sum(jnp.exp(scores - highest), axis=-1, keepdims=True))
        weights = jnp.exp(scores - log_total)
        weight_half = to_half(weights)
        attended = to_half(jnp.einsum('hjrk,khd->rhjd', weight_half, value_block))
        row_dot = jnp.einsum('rhjd,rhjd->hjr', attended, grad_block)
        weight_grad = jnp.einsum('rhjd,khd->hjrk', grad_block, value_block)
        score_grad = to_half(weights * (weight_grad - row_dot[..., None]))
        grad_query = SCORE_SCALE * jnp.einsum('hjrk,khd->rhjd', score_grad, key_block)
        grad_keys = split_round((SCORE_SCALE * jnp.einsum('hjrk,rhjd->khd', score_grad, query_block)).reshape(span, width))
        grad_values = split_round(jnp.einsum('hjrk,rhjd->khd', weight_half, grad_block).reshape(span, width))
        acc_keys = lax.dynamic_update_slice_in_dim(acc_keys, lax.dynamic_slice_in_dim(acc_keys, start, span, 0) + grad_keys, start, 0)
        acc_values = lax.dynamic_update_slice_in_dim(acc_values, lax.dynamic_slice_in_dim(acc_values, start, span, 0) + grad_values, start, 0)
        return (acc_keys, acc_values), grad_query.reshape(ROWS, HEADS * HEAD_DIM).astype(jnp.bfloat16)

    empty = jnp.zeros((WINDOW + SEQ, width), jnp.float32)
    (acc_keys, acc_values), query_blocks = lax.scan(step, (empty, empty), jnp.arange(SEQ // ROWS, dtype=jnp.int32))
    return (query_blocks.reshape(SEQ, HEADS * HEAD_DIM), acc_keys[WINDOW:].astype(jnp.bfloat16), acc_values[WINDOW:].astype(jnp.bfloat16))


def reference(query_rows, key_rows, value_rows, finished_grad, doc_lengths):
    arriving = jnp.roll(finished_grad, -1, axis=0)

    def one_section(items):
        return section_grads(items[0], items[1], items[2], items[3], doc_lengths)

    query_grad, key_grad, value_grad = lax.map(one_section, (query_rows, key_rows, value_rows, arriving))
    return (query_grad, key_grad, value_grad)
```

```python
import functools
import math

import jax
import jax.numpy as jnp
from jax import lax
from jax.experimental import pallas as pl
from jax.experimental.pallas import tpu as pltpu
from jax.sharding import PartitionSpec as P

WINDOW = 1024
KV_HEADS = 8
CORES = 2
TILE = 128

SCORE_SCALE = 168.0 ** (-0.5)
SCORE_SCALE_LOG2 = SCORE_SCALE * math.log2(math.e)
MESH = pl.DeviceIdType.MESH


def kernel(
    sections, chips,
    docs, q_in, k_in, v_in, o_in,
    dq_out, dk_out, dv_out,
    q_buf, o_buf, kv_buf, kt_buf, bias_buf, acc_k, acc_v, term_buf, got_buf, dq_buf,
    q_send, q_recv, o_send, o_recv, kv_send, kv_recv, g_send, g_recv, dq_send, dq_recv, dq_local,
):
    local_heads, chip_rows, group_width = q_buf.shape
    head_size = kt_buf.shape[0]
    rows = chip_rows // CORES
    reach = WINDOW // chip_rows
    own_start = reach * chip_rows
    width = WINDOW + TILE
    tiles = chip_rows // TILE
    sec = lax.axis_index("section")
    rank = lax.axis_index("ctx")
    chip = rank // CORES
    core = rank % CORES
    other = 1 - core
    sibling = chip * CORES + other
    sec_from = lax.rem(sec + 1, sections)
    sec_to = lax.rem(sec + sections - 1, sections)

    barrier = pltpu.get_barrier_semaphore()

    def greet(section, ctx):
        pl.semaphore_signal(barrier, inc=1, device_id=(section, ctx), device_id_type=MESH)

    greet(sec, sibling)
    for t in range(CORES):
        greet(sec_from, chip * CORES + t)
        greet(sec_to, chip * CORES + t)
    for away in range(1, reach + 1):
        @pl.when(chip >= away)
        def _():
            for t in range(CORES):
                greet(sec, (chip - away) * CORES + t)

        @pl.when(chip + away < chips)
        def _():
            for t in range(CORES):
                greet(sec, (chip + away) * CORES + t)
    peers = jnp.int32(1 + 2 * CORES)
    for away in range(1, reach + 1):
        peers = peers + jnp.where(chip >= away, CORES, 0) + jnp.where(chip + away < chips, CORES, 0)
    pl.semaphore_wait(barrier, peers)

    def aligned(start, size):
        return pl.ds(pl.multiple_of(start, size), size)

    def rows_of(c):
        return aligned(c * rows, rows)

    def group_cols(h, t):
        return aligned((t * local_heads + h) * group_width, group_width)

    def head_cols(h, t):
        return aligned((t * local_heads + h) * head_size, head_size)

    def copy_o(h, t, from_core):
        return pltpu.make_async_remote_copy(
            src_ref=o_in.at[0, :, group_cols(h, t)],
            dst_ref=o_buf.at[h, rows_of(from_core), :],
            send_sem=o_send.at[h, t],
            recv_sem=o_recv.at[h, from_core],
            device_id=(sec_to, chip * CORES + t),
            device_id_type=MESH,
        )

    def copy_q_sibling(h, from_core):
        return pltpu.make_async_remote_copy(
            src_ref=q_in.at[0, :, group_cols(h, other)],
            dst_ref=q_buf.at[h, rows_of(from_core), :],
            send_sem=q_send.at[h],
            recv_sem=q_recv.at[h, 1],
            device_id=(sec, sibling),
            device_id_type=MESH,
        )

    def copy_q_own(h):
        return pltpu.make_async_copy(
            q_in.at[0, :, group_cols(h, core)], q_buf.at[h, rows_of(core), :], q_recv.at[h, 0]
        )

    def kv_rows(away, c):
        return aligned((reach - away) * chip_rows + c * rows, rows)

    def copy_kv(h, which, away, t, from_core):
        source = (k_in, v_in)[which]
        return pltpu.make_async_remote_copy(
            src_ref=source.at[0, :, head_cols(h, t)],
            dst_ref=kv_buf.at[h, which, kv_rows(away, from_core), :],
            send_sem=kv_send.at[h, which, away * CORES + t],
            recv_sem=kv_recv.at[h, which, away * CORES + from_core],
            device_id=(sec, (chip + away) * CORES + t),
            device_id_type=MESH,
        )

    def copy_kv_own(h, which):
        source = (k_in, v_in)[which]
        return pltpu.make_async_copy(
            source.at[0, :, head_cols(h, core)],
            kv_buf.at[h, which, kv_rows(0, core), :],
            kv_recv.at[h, which, core],
        )

    def copy_term(h, away, t):
        return pltpu.make_async_remote_copy(
            src_ref=term_buf.at[h, :, kv_rows(away, t), :],
            dst_ref=got_buf.at[away, core * local_heads + h],
            send_sem=g_send.at[h, away * CORES + t],
            recv_sem=g_recv.at[away, core * local_heads + h],
            device_id=(sec, (chip - away) * CORES + t),
            device_id_type=MESH,
        )

    def wait_term(g, away):
        pltpu.make_async_remote_copy(
            src_ref=term_buf.at[0, :, pl.ds(0, rows), :],
            dst_ref=got_buf.at[away, g],
            send_sem=g_send.at[0, 0],
            recv_sem=g_recv.at[away, g],
            device_id=(sec, sibling),
            device_id_type=MESH,
        ).wait_recv()

    def copy_term_own(h):
        return pltpu.make_async_copy(
            term_buf.at[h, :, kv_rows(0, core), :],
            got_buf.at[0, core * local_heads + h],
            g_recv.at[0, core * local_heads + h],
        )

    def copy_dq_sibling(h, for_core):
        return pltpu.make_async_remote_copy(
            src_ref=dq_buf.at[h, rows_of(for_core), :],
            dst_ref=dq_out.at[0, :, group_cols(h, 1 - for_core)],
            send_sem=dq_send.at[h],
            recv_sem=dq_recv.at[h],
            device_id=(sec, sibling),
            device_id_type=MESH,
        )

    def copy_dq_own(h):
        return pltpu.make_async_copy(
            dq_buf.at[h, rows_of(core), :], dq_out.at[0, :, group_cols(h, core)], dq_local.at[h]
        )

    @pl.loop(0, local_heads)
    def _(h):
        for t in range(CORES):
            copy_o(h, t, core).start()
        for which in range(2):
            for away in range(1, reach + 1):
                @pl.when(chip + away < chips)
                def _():
                    for t in range(CORES):
                        copy_kv(h, which, away, t, core).start()
        copy_q_sibling(h, core).start()
        copy_q_own(h).start()
        for which in range(2):
            copy_kv(h, which, 0, other, core).start()
            copy_kv_own(h, which).start()

    for away in range(1, reach + 1):
        @pl.when(chip < away)
        def _():
            kv_buf[:, :, pl.ds((reach - away) * chip_rows, chip_rows), :] = jnp.zeros(
                (local_heads, 2, chip_rows, head_size), kv_buf.dtype
            )

        @pl.when(chip + away >= chips)
        def _():
            got_buf[away] = jnp.zeros(got_buf.shape[1:], got_buf.dtype)

    for tile in range(tiles):
        query_pos = chip * chip_rows + tile * TILE + lax.broadcasted_iota(jnp.int32, (1, TILE), 1)
        lowest = query_pos - (WINDOW - 1)
        end = jnp.int32(0)
        lowest = jnp.maximum(lowest, 0)
        for d in range(docs.shape[0]):
            end = end + docs[d]
            lowest = jnp.maximum(lowest, jnp.where(query_pos >= end, end, 0))
        key_pos = (
            chip * chip_rows - WINDOW + tile * TILE
            + lax.broadcasted_iota(jnp.int32, (width, TILE), 0)
        )
        bias_buf[tile] = jnp.where(
            (key_pos <= query_pos) & (key_pos >= lowest), 0.0, -jnp.inf
        ).astype(jnp.float32)

    def two_heads(block):
        return jnp.concatenate([block[:, :head_size], block[:, head_size:]], axis=0)

    @pl.loop(0, local_heads)
    def _(h):
        copy_q_own(h).wait()
        copy_q_sibling(h, other).wait_recv()
        for which in range(2):
            copy_kv_own(h, which).wait()
            copy_kv(h, which, 0, other, other).wait_recv()
        for c in range(CORES):
            copy_o(h, c, c).wait_recv()
        for away in range(1, reach + 1):
            @pl.when(chip >= away)
            def _():
                for which in range(2):
                    for c in range(CORES):
                        copy_kv(h, which, away, c, c).wait_recv()

        kt_buf[...] = kv_buf[h, 0].T
        acc_k[...] = jnp.zeros_like(acc_k)
        acc_v[...] = jnp.zeros_like(acc_v)

        @pl.loop(0, tiles)
        def _(tile):
            span = pl.ds(pl.multiple_of(tile * TILE, TILE), width)
            here = aligned(tile * TILE, TILE)
            keys = kv_buf[h, 0, span, :]
            values = kv_buf[h, 1, span, :]
            queries = two_heads(q_buf[h, here, :])
            grads = two_heads(o_buf[h, here, :])
            bias = bias_buf[tile]
            nt = (((1,), (1,)), ((), ()))
            scores = lax.dot_general(keys, queries, nt, preferred_element_type=jnp.float32)
            scores = scores * SCORE_SCALE_LOG2 + jnp.concatenate([bias, bias], axis=1)
            highest = jnp.max(scores, axis=0, keepdims=True)
            raised = jnp.exp2(scores - highest)
            weights = raised * (1.0 / jnp.sum(raised, axis=0, keepdims=True))
            weight_grad = lax.dot_general(values, grads, nt, preferred_element_type=jnp.float32)
            row_dot = jnp.sum(weights * weight_grad, axis=0, keepdims=True)
            score_grad = (weights * (weight_grad - row_dot)).astype(jnp.bfloat16)
            weight_half = weights.astype(jnp.bfloat16)
            acc_v[span, :] += jnp.dot(weight_half, grads, preferred_element_type=jnp.float32)
            acc_k[span, :] += jnp.dot(score_grad, queries, preferred_element_type=jnp.float32)
            back = jnp.dot(kt_buf[:, span], score_grad, preferred_element_type=jnp.float32)
            back = (back * SCORE_SCALE).T.astype(jnp.bfloat16)
            dq_buf[h, here, :] = jnp.concatenate([back[:TILE], back[TILE:]], axis=1)

        term_buf[h, 0] = (acc_k[...] * SCORE_SCALE).astype(jnp.bfloat16)
        term_buf[h, 1] = acc_v[...].astype(jnp.bfloat16)
        for away in range(1, reach + 1):
            @pl.when(chip >= away)
            def _():
                for t in range(CORES):
                    copy_term(h, away, t).start()
        copy_term(h, 0, other).start()
        copy_term_own(h).start()
        copy_dq_sibling(h, other).start()
        copy_dq_own(h).start()

    @pl.loop(0, local_heads)
    def _(h):
        copy_term_own(h).wait()
        wait_term(other * local_heads + h, 0)
        for away in range(1, reach + 1):
            @pl.when(chip + away < chips)
            def _():
                for t in range(CORES):
                    wait_term(t * local_heads + h, away)
        for t in range(CORES):
            g = t * local_heads + h
            total = got_buf[0, g].astype(jnp.float32)
            for away in range(1, reach + 1):
                total = total + got_buf[away, g].astype(jnp.float32)
            dk_out[0, :, head_cols(h, t)] = total[0].astype(jnp.bfloat16)
            dv_out[0, :, head_cols(h, t)] = total[1].astype(jnp.bfloat16)

    @pl.loop(0, local_heads)
    def _(h):
        copy_dq_own(h).wait()
        copy_dq_sibling(h, core).wait_recv()
        copy_dq_sibling(h, other).wait_send()
        copy_q_sibling(h, core).wait_send()
        for t in range(CORES):
            copy_o(h, t, core).wait_send()
        for which in range(2):
            copy_kv(h, which, 0, other, core).wait_send()
        copy_term(h, 0, other).wait_send()
        for away in range(1, reach + 1):
            @pl.when(chip + away < chips)
            def _():
                for which in range(2):
                    for t in range(CORES):
                        copy_kv(h, which, away, t, core).wait_send()

            @pl.when(chip >= away)
            def _():
                for t in range(CORES):
                    copy_term(h, away, t).wait_send()


def local(sections, chips, query_rows, key_rows, value_rows, finished_grad, doc_lengths):
    rows = query_rows.shape[1]
    kv_width = key_rows.shape[2]
    head_size = kv_width // KV_HEADS
    group_width = query_rows.shape[2] // KV_HEADS
    local_heads = KV_HEADS // CORES
    chip_rows = CORES * rows
    reach = WINDOW // chip_rows
    span = WINDOW + chip_rows
    half = jnp.bfloat16
    dma = pltpu.SemaphoreType.DMA
    anywhere = pl.BlockSpec(memory_space=pl.ANY)
    in_vmem = pl.BlockSpec(memory_space=pltpu.VMEM)
    pairs = 2 * (KV_HEADS // 2) * chip_rows * (WINDOW + TILE)
    return pl.pallas_call(
        functools.partial(kernel, sections, chips),
        out_shape=(
            jax.ShapeDtypeStruct(query_rows.shape, half),
            jax.ShapeDtypeStruct(key_rows.shape, half),
            jax.ShapeDtypeStruct(value_rows.shape, half),
        ),
        in_specs=[pl.BlockSpec(memory_space=pltpu.SMEM)] + [anywhere] * 4,
        out_specs=(anywhere, in_vmem, in_vmem),
        scratch_shapes=[
            pltpu.VMEM((local_heads, chip_rows, group_width), half),
            pltpu.VMEM((local_heads, chip_rows, group_width), half),
            pltpu.VMEM((local_heads, 2, span, head_size), half),
            pltpu.VMEM((head_size, span), half),
            pltpu.VMEM((chip_rows // TILE, WINDOW + TILE, TILE), jnp.float32),
            pltpu.VMEM((span, head_size), jnp.float32),
            pltpu.VMEM((span, head_size), jnp.float32),
            pltpu.VMEM((local_heads, 2, span, head_size), half),
            pltpu.VMEM((reach + 1, KV_HEADS, 2, rows, head_size), half),
            pltpu.VMEM((local_heads, chip_rows, group_width), half),
            dma((local_heads,)),
            dma((local_heads, 2)),
            dma((local_heads, CORES)),
            dma((local_heads, CORES)),
            dma((local_heads, 2, (reach + 1) * CORES)),
            dma((local_heads, 2, (reach + 1) * CORES)),
            dma((local_heads, (reach + 1) * CORES)),
            dma((reach + 1, KV_HEADS)),
            dma((local_heads,)),
            dma((local_heads,)),
            dma((local_heads,)),
        ],
        compiler_params=pltpu.CompilerParams(
            collective_id=0, has_side_effects=True, vmem_limit_bytes=48 * 1024 * 1024
        ),
        cost_estimate=pl.CostEstimate(
            flops=10 * pairs * head_size, bytes_accessed=8 * 1024 * 1024, transcendentals=pairs
        ),
    )(doc_lengths, query_rows, key_rows, value_rows, finished_grad)


def solution(mesh):
    spec = P("section", "ctx", None)
    return jax.shard_map(
        functools.partial(local, mesh.shape["section"], mesh.shape["ctx"] // CORES),
        mesh=mesh,
        in_specs=(spec, spec, spec, spec, P()),
        out_specs=(spec, spec, spec),
        check_vma=False,
    )
```

```python
import functools
import math

import jax
import jax.numpy as jnp
from jax import lax
from jax.experimental import pallas as pl
from jax.experimental.pallas import tpu as pltpu
from jax.sharding import PartitionSpec as P

WINDOW = 1024
KV_HEADS = 8
CORES = 2
TILE = 128

SCORE_SCALE = 168.0 ** (-0.5)
SCORE_SCALE_LOG2 = SCORE_SCALE * math.log2(math.e)
MESH = pl.DeviceIdType.MESH


def kernel(
    sections, chips,
    docs, q_in, k_in, v_in, o_in,
    dq_out, dk_out, dv_out,
    q_buf, o_buf, kv_buf, kt_buf, bias_buf, acc_k, acc_v, term_buf, got_buf, dq_buf,
    q_send, q_recv, o_send, o_recv, kv_send, kv_recv, g_send, g_recv, dq_send, dq_recv, dq_local, relay_send, relay_recv,
):
    local_heads, chip_rows, group_width = q_buf.shape
    head_size = kt_buf.shape[0]
    rows = chip_rows // CORES
    reach = WINDOW // chip_rows
    own_start = reach * chip_rows
    width = WINDOW + TILE
    tiles = chip_rows // TILE
    sec = lax.axis_index("section")
    rank = lax.axis_index("ctx")
    chip = rank // CORES
    core = rank % CORES
    other = 1 - core
    sibling = chip * CORES + other
    sec_from = lax.rem(sec + 1, sections)
    sec_to = lax.rem(sec + sections - 1, sections)

    relayed = chips == 4 and reach >= 2

    def sends_to(away):
        sends = chip + away < chips
        return sends & (chip != 1) if relayed and away == 1 else sends

    def gets_from(away):
        gets = chip >= away
        return gets & (chip != 2) if relayed and away == 1 else gets

    barrier = pltpu.get_barrier_semaphore()

    def greet(section, ctx):
        pl.semaphore_signal(barrier, inc=1, device_id=(section, ctx), device_id_type=MESH)

    greet(sec, sibling)
    for t in range(CORES):
        greet(sec_from, chip * CORES + t)
        greet(sec_to, chip * CORES + t)
    for away in range(1, reach + 1):
        @pl.when(chip >= away)
        def _():
            for t in range(CORES):
                greet(sec, (chip - away) * CORES + t)

        @pl.when(chip + away < chips)
        def _():
            for t in range(CORES):
                greet(sec, (chip + away) * CORES + t)
    peers = jnp.int32(1 + 2 * CORES)
    for away in range(1, reach + 1):
        peers = peers + jnp.where(chip >= away, CORES, 0) + jnp.where(chip + away < chips, CORES, 0)
    pl.semaphore_wait(barrier, peers)

    def aligned(start, size):
        return pl.ds(pl.multiple_of(start, size), size)

    def rows_of(c):
        return aligned(c * rows, rows)

    def group_cols(h, t):
        return aligned((t * local_heads + h) * group_width, group_width)

    def head_cols(h, t):
        return aligned((t * local_heads + h) * head_size, head_size)

    def copy_o(h, t, from_core):
        return pltpu.make_async_remote_copy(
            src_ref=o_in.at[0, :, group_cols(h, t)],
            dst_ref=o_buf.at[h, rows_of(from_core), :],
            send_sem=o_send.at[h, t],
            recv_sem=o_recv.at[h, from_core],
            device_id=(sec_to, chip * CORES + t),
            device_id_type=MESH,
        )

    def copy_q_sibling(h, from_core):
        return pltpu.make_async_remote_copy(
            src_ref=q_in.at[0, :, group_cols(h, other)],
            dst_ref=q_buf.at[h, rows_of(from_core), :],
            send_sem=q_send.at[h],
            recv_sem=q_recv.at[h, 1],
            device_id=(sec, sibling),
            device_id_type=MESH,
        )

    def copy_q_own(h):
        return pltpu.make_async_copy(
            q_in.at[0, :, group_cols(h, core)], q_buf.at[h, rows_of(core), :], q_recv.at[h, 0]
        )

    def kv_rows(away, c):
        return aligned((reach - away) * chip_rows + c * rows, rows)

    def copy_kv(h, which, away, t, from_core):
        source = (k_in, v_in)[which]
        return pltpu.make_async_remote_copy(
            src_ref=source.at[0, :, head_cols(h, t)],
            dst_ref=kv_buf.at[h, which, kv_rows(away, from_core), :],
            send_sem=kv_send.at[h, which, away * CORES + t],
            recv_sem=kv_recv.at[h, which, away * CORES + from_core],
            device_id=(sec, (chip + away) * CORES + t),
            device_id_type=MESH,
        )

    def copy_kv_own(h, which):
        source = (k_in, v_in)[which]
        return pltpu.make_async_copy(
            source.at[0, :, head_cols(h, core)],
            kv_buf.at[h, which, kv_rows(0, core), :],
            kv_recv.at[h, which, core],
        )

    def copy_relay(h):
        return pltpu.make_async_remote_copy(
            src_ref=kv_buf.at[h, :, pl.ds((reach - 2) * chip_rows, chip_rows), :],
            dst_ref=kv_buf.at[h, :, pl.ds((reach - 1) * chip_rows, chip_rows), :],
            send_sem=relay_send.at[h],
            recv_sem=relay_recv.at[h],
            device_id=(sec, (chip - 1) * CORES + core),
            device_id_type=MESH,
        )

    def copy_term(h, away, t):
        return pltpu.make_async_remote_copy(
            src_ref=term_buf.at[h, :, kv_rows(away, t), :],
            dst_ref=got_buf.at[away, core * local_heads + h],
            send_sem=g_send.at[h, away * CORES + t],
            recv_sem=g_recv.at[away, core * local_heads + h],
            device_id=(sec, (chip - away) * CORES + t),
            device_id_type=MESH,
        )

    def wait_term(g, away):
        pltpu.make_async_remote_copy(
            src_ref=term_buf.at[0, :, pl.ds(0, rows), :],
            dst_ref=got_buf.at[away, g],
            send_sem=g_send.at[0, 0],
            recv_sem=g_recv.at[away, g],
            device_id=(sec, sibling),
            device_id_type=MESH,
        ).wait_recv()

    def copy_term_own(h):
        return pltpu.make_async_copy(
            term_buf.at[h, :, kv_rows(0, core), :],
            got_buf.at[0, core * local_heads + h],
            g_recv.at[0, core * local_heads + h],
        )

    def copy_dq_sibling(h, for_core):
        return pltpu.make_async_remote_copy(
            src_ref=dq_buf.at[h, rows_of(for_core), :],
            dst_ref=dq_out.at[0, :, group_cols(h, 1 - for_core)],
            send_sem=dq_send.at[h],
            recv_sem=dq_recv.at[h],
            device_id=(sec, sibling),
            device_id_type=MESH,
        )

    def copy_dq_own(h):
        return pltpu.make_async_copy(
            dq_buf.at[h, rows_of(core), :], dq_out.at[0, :, group_cols(h, core)], dq_local.at[h]
        )

    @pl.loop(0, local_heads)
    def _(h):
        for t in range(CORES):
            copy_o(h, t, core).start()
        for which in range(2):
            for away in range(1, reach + 1):
                @pl.when(sends_to(away))
                def _():
                    for t in range(CORES):
                        copy_kv(h, which, away, t, core).start()
        copy_q_sibling(h, core).start()
        copy_q_own(h).start()
        for which in range(2):
            copy_kv(h, which, 0, other, core).start()
            copy_kv_own(h, which).start()

    for away in range(1, reach + 1):
        @pl.when(chip < away)
        def _():
            kv_buf[:, :, pl.ds((reach - away) * chip_rows, chip_rows), :] = jnp.zeros(
                (local_heads, 2, chip_rows, head_size), kv_buf.dtype
            )

        @pl.when(chip + away >= chips)
        def _():
            got_buf[away] = jnp.zeros(got_buf.shape[1:], got_buf.dtype)

    for tile in range(tiles):
        query_pos = chip * chip_rows + tile * TILE + lax.broadcasted_iota(jnp.int32, (1, TILE), 1)
        lowest = query_pos - (WINDOW - 1)
        end = jnp.int32(0)
        lowest = jnp.maximum(lowest, 0)
        for d in range(docs.shape[0]):
            end = end + docs[d]
            lowest = jnp.maximum(lowest, jnp.where(query_pos >= end, end, 0))
        key_pos = (
            chip * chip_rows - WINDOW + tile * TILE
            + lax.broadcasted_iota(jnp.int32, (width, TILE), 0)
        )
        bias_buf[tile] = jnp.where(
            (key_pos <= query_pos) & (key_pos >= lowest), 0.0, -jnp.inf
        ).astype(jnp.float32)

    def two_heads(block):
        return jnp.concatenate([block[:, :head_size], block[:, head_size:]], axis=0)

    @pl.loop(0, local_heads)
    def _(h):
        for away in range(reach, 0, -1):
            @pl.when(gets_from(away))
            def _():
                for which in range(2):
                    for c in range(CORES):
                        copy_kv(h, which, away, c, c).wait_recv()

            if relayed and away == 2:
                @pl.when(chip == 3)
                def _():
                    copy_relay(h).start()

        copy_q_own(h).wait()
        copy_q_sibling(h, other).wait_recv()
        for which in range(2):
            copy_kv_own(h, which).wait()
            copy_kv(h, which, 0, other, other).wait_recv()
        for c in range(CORES):
            copy_o(h, c, c).wait_recv()
        if relayed:
            @pl.when(chip == 2)
            def _():
                copy_relay(h).wait_recv()

        kt_buf[...] = kv_buf[h, 0].T
        acc_k[...] = jnp.zeros_like(acc_k)
        acc_v[...] = jnp.zeros_like(acc_v)

        @pl.loop(0, tiles)
        def _(tile):
            span = pl.ds(pl.multiple_of(tile * TILE, TILE), width)
            here = aligned(tile * TILE, TILE)
            keys = kv_buf[h, 0, span, :]
            values = kv_buf[h, 1, span, :]
            queries = two_heads(q_buf[h, here, :])
            grads = two_heads(o_buf[h, here, :])
            bias = bias_buf[tile]
            nt = (((1,), (1,)), ((), ()))
            scores = lax.dot_general(keys, queries, nt, preferred_element_type=jnp.float32)
            scores = scores * SCORE_SCALE_LOG2 + jnp.concatenate([bias, bias], axis=1)
            highest = jnp.max(scores, axis=0, keepdims=True)
            raised = jnp.exp2(scores - highest)
            weights = raised * (1.0 / jnp.sum(raised, axis=0, keepdims=True))
            weight_grad = lax.dot_general(values, grads, nt, preferred_element_type=jnp.float32)
            row_dot = jnp.sum(weights * weight_grad, axis=0, keepdims=True)
            score_grad = (weights * (weight_grad - row_dot)).astype(jnp.bfloat16)
            weight_half = weights.astype(jnp.bfloat16)
            acc_v[span, :] += jnp.dot(weight_half, grads, preferred_element_type=jnp.float32)
            acc_k[span, :] += jnp.dot(score_grad, queries, preferred_element_type=jnp.float32)
            back = jnp.dot(kt_buf[:, span], score_grad, preferred_element_type=jnp.float32)
            back = (back * SCORE_SCALE).T.astype(jnp.bfloat16)
            dq_buf[h, here, :] = jnp.concatenate([back[:TILE], back[TILE:]], axis=1)

        term_buf[h, 0] = (acc_k[...] * SCORE_SCALE).astype(jnp.bfloat16)
        term_buf[h, 1] = acc_v[...].astype(jnp.bfloat16)
        for away in range(1, reach + 1):
            @pl.when(chip >= away)
            def _():
                for t in range(CORES):
                    copy_term(h, away, t).start()
        copy_term(h, 0, other).start()
        copy_term_own(h).start()
        copy_dq_sibling(h, other).start()
        copy_dq_own(h).start()

    @pl.loop(0, local_heads)
    def _(h):
        copy_term_own(h).wait()
        wait_term(other * local_heads + h, 0)
        for away in range(1, reach + 1):
            @pl.when(chip + away < chips)
            def _():
                for t in range(CORES):
                    wait_term(t * local_heads + h, away)
        for t in range(CORES):
            g = t * local_heads + h
            total = got_buf[0, g].astype(jnp.float32)
            for away in range(1, reach + 1):
                total = total + got_buf[away, g].astype(jnp.float32)
            dk_out[0, :, head_cols(h, t)] = total[0].astype(jnp.bfloat16)
            dv_out[0, :, head_cols(h, t)] = total[1].astype(jnp.bfloat16)

    @pl.loop(0, local_heads)
    def _(h):
        copy_dq_own(h).wait()
        copy_dq_sibling(h, core).wait_recv()
        copy_dq_sibling(h, other).wait_send()
        copy_q_sibling(h, core).wait_send()
        for t in range(CORES):
            copy_o(h, t, core).wait_send()
        for which in range(2):
            copy_kv(h, which, 0, other, core).wait_send()
        copy_term(h, 0, other).wait_send()
        if relayed:
            @pl.when(chip == 3)
            def _():
                copy_relay(h).wait_send()

        for away in range(1, reach + 1):
            @pl.when(sends_to(away))
            def _():
                for which in range(2):
                    for t in range(CORES):
                        copy_kv(h, which, away, t, core).wait_send()

            @pl.when(chip >= away)
            def _():
                for t in range(CORES):
                    copy_term(h, away, t).wait_send()


def local(sections, chips, query_rows, key_rows, value_rows, finished_grad, doc_lengths):
    rows = query_rows.shape[1]
    kv_width = key_rows.shape[2]
    head_size = kv_width // KV_HEADS
    group_width = query_rows.shape[2] // KV_HEADS
    local_heads = KV_HEADS // CORES
    chip_rows = CORES * rows
    reach = WINDOW // chip_rows
    span = WINDOW + chip_rows
    half = jnp.bfloat16
    dma = pltpu.SemaphoreType.DMA
    anywhere = pl.BlockSpec(memory_space=pl.ANY)
    in_vmem = pl.BlockSpec(memory_space=pltpu.VMEM)
    pairs = 2 * (KV_HEADS // 2) * chip_rows * (WINDOW + TILE)
    return pl.pallas_call(
        functools.partial(kernel, sections, chips),
        out_shape=(
            jax.ShapeDtypeStruct(query_rows.shape, half),
            jax.ShapeDtypeStruct(key_rows.shape, half),
            jax.ShapeDtypeStruct(value_rows.shape, half),
        ),
        in_specs=[pl.BlockSpec(memory_space=pltpu.SMEM)] + [anywhere] * 4,
        out_specs=(anywhere, in_vmem, in_vmem),
        scratch_shapes=[
            pltpu.VMEM((local_heads, chip_rows, group_width), half),
            pltpu.VMEM((local_heads, chip_rows, group_width), half),
            pltpu.VMEM((local_heads, 2, span, head_size), half),
            pltpu.VMEM((head_size, span), half),
            pltpu.VMEM((chip_rows // TILE, WINDOW + TILE, TILE), jnp.float32),
            pltpu.VMEM((span, head_size), jnp.float32),
            pltpu.VMEM((span, head_size), jnp.float32),
            pltpu.VMEM((local_heads, 2, span, head_size), half),
            pltpu.VMEM((reach + 1, KV_HEADS, 2, rows, head_size), half),
            pltpu.VMEM((local_heads, chip_rows, group_width), half),
            dma((local_heads,)),
            dma((local_heads, 2)),
            dma((local_heads, CORES)),
            dma((local_heads, CORES)),
            dma((local_heads, 2, (reach + 1) * CORES)),
            dma((local_heads, 2, (reach + 1) * CORES)),
            dma((local_heads, (reach + 1) * CORES)),
            dma((reach + 1, KV_HEADS)),
            dma((local_heads,)),
            dma((local_heads,)),
            dma((local_heads,)),
            dma((local_heads,)),
            dma((local_heads,)),
        ],
        compiler_params=pltpu.CompilerParams(
            collective_id=0, has_side_effects=True, vmem_limit_bytes=63 * 1024 * 1024
        ),
        cost_estimate=pl.CostEstimate(
            flops=10 * pairs * head_size, bytes_accessed=8 * 1024 * 1024, transcendentals=pairs
        ),
    )(doc_lengths, query_rows, key_rows, value_rows, finished_grad)


def solution(mesh):
    spec = P("section", "ctx", None)
    return jax.shard_map(
        functools.partial(local, mesh.shape["section"], mesh.shape["ctx"] // CORES),
        mesh=mesh,
        in_specs=(spec, spec, spec, spec, P()),
        out_specs=(spec, spec, spec),
        check_vma=False,
    )
```

```python
import functools
import math

import jax
import jax.numpy as jnp
from jax import lax
from jax.experimental import pallas as pl
from jax.experimental.pallas import tpu as pltpu
from jax.sharding import PartitionSpec as P

WINDOW = 1024
KV_HEADS = 8
CORES = 2
TILE = 128

SCORE_SCALE = 168.0 ** (-0.5)
SCORE_SCALE_LOG2 = SCORE_SCALE * math.log2(math.e)
MESH = pl.DeviceIdType.MESH


def kernel(
    sections, chips,
    docs, q_in, k_in, v_in, o_in,
    dq_out, dk_out, dv_out,
    q_buf, o_buf, kv_buf, kt_buf, bias_buf, acc_k, acc_v, term_buf, got_buf, dq_buf,
    q_send, q_recv, o_send, o_recv, kv_send, kv_recv, g_send, g_recv, dq_send, dq_recv, dq_local, relay_send, relay_recv,
):
    local_heads, chip_rows, group_width = q_buf.shape
    head_size = kt_buf.shape[0]
    rows = chip_rows // CORES
    reach = WINDOW // chip_rows
    own_start = reach * chip_rows
    width = WINDOW + TILE
    tiles = chip_rows // TILE
    sec = lax.axis_index("section")
    rank = lax.axis_index("ctx")
    chip = rank // CORES
    core = rank % CORES
    other = 1 - core
    sibling = chip * CORES + other
    sec_from = lax.rem(sec + 1, sections)
    sec_to = lax.rem(sec + sections - 1, sections)

    relayed = chips == 4 and reach >= 2

    def sends_to(away):
        sends = chip + away < chips
        return sends & (chip != 1) if relayed and away == 1 else sends

    def gets_from(away):
        gets = chip >= away
        return gets & (chip != 2) if relayed and away == 1 else gets

    barrier = pltpu.get_barrier_semaphore()

    def greet(section, ctx):
        pl.semaphore_signal(barrier, inc=1, device_id=(section, ctx), device_id_type=MESH)

    greet(sec, sibling)
    for t in range(CORES):
        greet(sec_from, chip * CORES + t)
        greet(sec_to, chip * CORES + t)
    for away in range(1, reach + 1):
        @pl.when(chip >= away)
        def _():
            for t in range(CORES):
                greet(sec, (chip - away) * CORES + t)

        @pl.when(chip + away < chips)
        def _():
            for t in range(CORES):
                greet(sec, (chip + away) * CORES + t)
    peers = jnp.int32(1 + 2 * CORES)
    for away in range(1, reach + 1):
        peers = peers + jnp.where(chip >= away, CORES, 0) + jnp.where(chip + away < chips, CORES, 0)
    pl.semaphore_wait(barrier, peers)

    def aligned(start, size):
        return pl.ds(pl.multiple_of(start, size), size)

    def rows_of(c):
        return aligned(c * rows, rows)

    def group_cols(h, t):
        return aligned((t * local_heads + h) * group_width, group_width)

    def head_cols(h, t):
        return aligned((t * local_heads + h) * head_size, head_size)

    def copy_o(h, t, from_core):
        return pltpu.make_async_remote_copy(
            src_ref=o_in.at[0, :, group_cols(h, t)],
            dst_ref=o_buf.at[h, rows_of(from_core), :],
            send_sem=o_send.at[h, t],
            recv_sem=o_recv.at[h, from_core],
            device_id=(sec_to, chip * CORES + t),
            device_id_type=MESH,
        )

    def copy_q_sibling(h, from_core):
        return pltpu.make_async_remote_copy(
            src_ref=q_in.at[0, :, group_cols(h, other)],
            dst_ref=q_buf.at[h, rows_of(from_core), :],
            send_sem=q_send.at[h],
            recv_sem=q_recv.at[h, 1],
            device_id=(sec, sibling),
            device_id_type=MESH,
        )

    def copy_q_own(h):
        return pltpu.make_async_copy(
            q_in.at[0, :, group_cols(h, core)], q_buf.at[h, rows_of(core), :], q_recv.at[h, 0]
        )

    def kv_rows(away, c):
        return aligned((reach - away) * chip_rows + c * rows, rows)

    def copy_kv(h, which, away, t, from_core):
        source = (k_in, v_in)[which]
        return pltpu.make_async_remote_copy(
            src_ref=source.at[0, :, head_cols(h, t)],
            dst_ref=kv_buf.at[h, which, kv_rows(away, from_core), :],
            send_sem=kv_send.at[h, which, away * CORES + t],
            recv_sem=kv_recv.at[h, which, away * CORES + from_core],
            device_id=(sec, (chip + away) * CORES + t),
            device_id_type=MESH,
        )

    def copy_kv_own(h, which):
        source = (k_in, v_in)[which]
        return pltpu.make_async_copy(
            source.at[0, :, head_cols(h, core)],
            kv_buf.at[h, which, kv_rows(0, core), :],
            kv_recv.at[h, which, core],
        )

    def copy_relay(h):
        return pltpu.make_async_remote_copy(
            src_ref=kv_buf.at[h, :, pl.ds((reach - 2) * chip_rows, chip_rows), :],
            dst_ref=kv_buf.at[h, :, pl.ds((reach - 1) * chip_rows, chip_rows), :],
            send_sem=relay_send.at[h],
            recv_sem=relay_recv.at[h],
            device_id=(sec, (chip - 1) * CORES + core),
            device_id_type=MESH,
        )

    def copy_term(h, away, t):
        return pltpu.make_async_remote_copy(
            src_ref=term_buf.at[h, :, kv_rows(away, t), :],
            dst_ref=got_buf.at[away, core * local_heads + h],
            send_sem=g_send.at[h, away * CORES + t],
            recv_sem=g_recv.at[away, core * local_heads + h],
            device_id=(sec, (chip - away) * CORES + t),
            device_id_type=MESH,
        )

    def wait_term(g, away):
        pltpu.make_async_remote_copy(
            src_ref=term_buf.at[0, :, pl.ds(0, rows), :],
            dst_ref=got_buf.at[away, g],
            send_sem=g_send.at[0, 0],
            recv_sem=g_recv.at[away, g],
            device_id=(sec, sibling),
            device_id_type=MESH,
        ).wait_recv()

    def copy_term_own(h):
        return pltpu.make_async_copy(
            term_buf.at[h, :, kv_rows(0, core), :],
            got_buf.at[0, core * local_heads + h],
            g_recv.at[0, core * local_heads + h],
        )

    def copy_dq_sibling(h, for_core):
        return pltpu.make_async_remote_copy(
            src_ref=dq_buf.at[h, rows_of(for_core), :],
            dst_ref=dq_out.at[0, :, group_cols(h, 1 - for_core)],
            send_sem=dq_send.at[h],
            recv_sem=dq_recv.at[h],
            device_id=(sec, sibling),
            device_id_type=MESH,
        )

    def copy_dq_own(h):
        return pltpu.make_async_copy(
            dq_buf.at[h, rows_of(core), :], dq_out.at[0, :, group_cols(h, core)], dq_local.at[h]
        )

    def send_head(h):
        for t in range(CORES):
            copy_o(h, t, core).start()
        for which in range(2):
            for away in range(1, reach + 1):
                @pl.when(sends_to(away))
                def _():
                    for t in range(CORES):
                        copy_kv(h, which, away, t, core).start()
        copy_q_sibling(h, core).start()
        copy_q_own(h).start()
        for which in range(2):
            copy_kv(h, which, 0, other, core).start()
            copy_kv_own(h, which).start()

    send_head(0)

    for away in range(1, reach + 1):
        @pl.when(chip < away)
        def _():
            kv_buf[:, :, pl.ds((reach - away) * chip_rows, chip_rows), :] = jnp.zeros(
                (local_heads, 2, chip_rows, head_size), kv_buf.dtype
            )

        @pl.when(chip + away >= chips)
        def _():
            got_buf[away] = jnp.zeros(got_buf.shape[1:], got_buf.dtype)

    for tile in range(tiles):
        query_pos = chip * chip_rows + tile * TILE + lax.broadcasted_iota(jnp.int32, (1, TILE), 1)
        lowest = query_pos - (WINDOW - 1)
        end = jnp.int32(0)
        lowest = jnp.maximum(lowest, 0)
        for d in range(docs.shape[0]):
            end = end + docs[d]
            lowest = jnp.maximum(lowest, jnp.where(query_pos >= end, end, 0))
        key_pos = (
            chip * chip_rows - WINDOW + tile * TILE
            + lax.broadcasted_iota(jnp.int32, (width, TILE), 0)
        )
        bias_buf[tile] = jnp.where(
            (key_pos <= query_pos) & (key_pos >= lowest), 0.0, -jnp.inf
        ).astype(jnp.float32)

    def two_heads(block):
        return jnp.concatenate([block[:, :head_size], block[:, head_size:]], axis=0)

    @pl.loop(0, local_heads)
    def _(h):
        for away in range(reach, 0, -1):
            @pl.when(gets_from(away))
            def _():
                for which in range(2):
                    for c in range(CORES):
                        copy_kv(h, which, away, c, c).wait_recv()

            if relayed and away == 2:
                @pl.when(chip == 3)
                def _():
                    copy_relay(h).start()

        copy_q_own(h).wait()
        copy_q_sibling(h, other).wait_recv()
        for which in range(2):
            copy_kv_own(h, which).wait()
            copy_kv(h, which, 0, other, other).wait_recv()
        for c in range(CORES):
            copy_o(h, c, c).wait_recv()
        if relayed:
            @pl.when(chip == 2)
            def _():
                copy_relay(h).wait_recv()

        @pl.when(h + 1 < local_heads)
        def _():
            send_head(h + 1)

        kt_buf[...] = kv_buf[h, 0].T
        acc_k[...] = jnp.zeros_like(acc_k)
        acc_v[...] = jnp.zeros_like(acc_v)

        @pl.loop(0, tiles)
        def _(tile):
            span = pl.ds(pl.multiple_of(tile * TILE, TILE), width)
            here = aligned(tile * TILE, TILE)
            keys = kv_buf[h, 0, span, :]
            values = kv_buf[h, 1, span, :]
            queries = two_heads(q_buf[h, here, :])
            grads = two_heads(o_buf[h, here, :])
            bias = bias_buf[tile]
            nt = (((1,), (1,)), ((), ()))
            scores = lax.dot_general(keys, queries, nt, preferred_element_type=jnp.float32)
            scores = scores * SCORE_SCALE_LOG2 + jnp.concatenate([bias, bias], axis=1)
            highest = jnp.max(scores, axis=0, keepdims=True)
            raised = jnp.exp2(scores - highest)
            weights = raised * (1.0 / jnp.sum(raised, axis=0, keepdims=True))
            weight_grad = lax.dot_general(values, grads, nt, preferred_element_type=jnp.float32)
            row_dot = jnp.sum(weights * weight_grad, axis=0, keepdims=True)
            score_grad = (weights * (weight_grad - row_dot)).astype(jnp.bfloat16)
            weight_half = weights.astype(jnp.bfloat16)
            acc_v[span, :] += jnp.dot(weight_half, grads, preferred_element_type=jnp.float32)
            acc_k[span, :] += jnp.dot(score_grad, queries, preferred_element_type=jnp.float32)
            back = jnp.dot(kt_buf[:, span], score_grad, preferred_element_type=jnp.float32)
            back = (back * SCORE_SCALE).T.astype(jnp.bfloat16)
            dq_buf[h, here, :] = jnp.concatenate([back[:TILE], back[TILE:]], axis=1)

        term_buf[h, 0] = (acc_k[...] * SCORE_SCALE).astype(jnp.bfloat16)
        term_buf[h, 1] = acc_v[...].astype(jnp.bfloat16)
        for away in range(1, reach + 1):
            @pl.when(chip >= away)
            def _():
                for t in range(CORES):
                    copy_term(h, away, t).start()
        copy_term(h, 0, other).start()
        copy_term_own(h).start()
        copy_dq_sibling(h, other).start()
        copy_dq_own(h).start()

    @pl.loop(0, local_heads)
    def _(h):
        copy_term_own(h).wait()
        wait_term(other * local_heads + h, 0)
        for away in range(1, reach + 1):
            @pl.when(chip + away < chips)
            def _():
                for t in range(CORES):
                    wait_term(t * local_heads + h, away)
        for t in range(CORES):
            g = t * local_heads + h
            total = got_buf[0, g].astype(jnp.float32)
            for away in range(1, reach + 1):
                total = total + got_buf[away, g].astype(jnp.float32)
            dk_out[0, :, head_cols(h, t)] = total[0].astype(jnp.bfloat16)
            dv_out[0, :, head_cols(h, t)] = total[1].astype(jnp.bfloat16)

    @pl.loop(0, local_heads)
    def _(h):
        copy_dq_own(h).wait()
        copy_dq_sibling(h, core).wait_recv()
        copy_dq_sibling(h, other).wait_send()
        copy_q_sibling(h, core).wait_send()
        for t in range(CORES):
            copy_o(h, t, core).wait_send()
        for which in range(2):
            copy_kv(h, which, 0, other, core).wait_send()
        copy_term(h, 0, other).wait_send()
        if relayed:
            @pl.when(chip == 3)
            def _():
                copy_relay(h).wait_send()

        for away in range(1, reach + 1):
            @pl.when(sends_to(away))
            def _():
                for which in range(2):
                    for t in range(CORES):
                        copy_kv(h, which, away, t, core).wait_send()

            @pl.when(chip >= away)
            def _():
                for t in range(CORES):
                    copy_term(h, away, t).wait_send()


def local(sections, chips, query_rows, key_rows, value_rows, finished_grad, doc_lengths):
    rows = query_rows.shape[1]
    kv_width = key_rows.shape[2]
    head_size = kv_width // KV_HEADS
    group_width = query_rows.shape[2] // KV_HEADS
    local_heads = KV_HEADS // CORES
    chip_rows = CORES * rows
    reach = WINDOW // chip_rows
    span = WINDOW + chip_rows
    half = jnp.bfloat16
    dma = pltpu.SemaphoreType.DMA
    anywhere = pl.BlockSpec(memory_space=pl.ANY)
    in_vmem = pl.BlockSpec(memory_space=pltpu.VMEM)
    pairs = 2 * (KV_HEADS // 2) * chip_rows * (WINDOW + TILE)
    return pl.pallas_call(
        functools.partial(kernel, sections, chips),
        out_shape=(
            jax.ShapeDtypeStruct(query_rows.shape, half),
            jax.ShapeDtypeStruct(key_rows.shape, half),
            jax.ShapeDtypeStruct(value_rows.shape, half),
        ),
        in_specs=[pl.BlockSpec(memory_space=pltpu.SMEM)] + [anywhere] * 4,
        out_specs=(anywhere, in_vmem, in_vmem),
        scratch_shapes=[
            pltpu.VMEM((local_heads, chip_rows, group_width), half),
            pltpu.VMEM((local_heads, chip_rows, group_width), half),
            pltpu.VMEM((local_heads, 2, span, head_size), half),
            pltpu.VMEM((head_size, span), half),
            pltpu.VMEM((chip_rows // TILE, WINDOW + TILE, TILE), jnp.float32),
            pltpu.VMEM((span, head_size), jnp.float32),
            pltpu.VMEM((span, head_size), jnp.float32),
            pltpu.VMEM((local_heads, 2, span, head_size), half),
            pltpu.VMEM((reach + 1, KV_HEADS, 2, rows, head_size), half),
            pltpu.VMEM((local_heads, chip_rows, group_width), half),
            dma((local_heads,)),
            dma((local_heads, 2)),
            dma((local_heads, CORES)),
            dma((local_heads, CORES)),
            dma((local_heads, 2, (reach + 1) * CORES)),
            dma((local_heads, 2, (reach + 1) * CORES)),
            dma((local_heads, (reach + 1) * CORES)),
            dma((reach + 1, KV_HEADS)),
            dma((local_heads,)),
            dma((local_heads,)),
            dma((local_heads,)),
            dma((local_heads,)),
            dma((local_heads,)),
        ],
        compiler_params=pltpu.CompilerParams(
            collective_id=0, has_side_effects=True, vmem_limit_bytes=63 * 1024 * 1024
        ),
        cost_estimate=pl.CostEstimate(
            flops=10 * pairs * head_size, bytes_accessed=8 * 1024 * 1024, transcendentals=pairs
        ),
    )(doc_lengths, query_rows, key_rows, value_rows, finished_grad)


def solution(mesh):
    spec = P("section", "ctx", None)
    return jax.shard_map(
        functools.partial(local, mesh.shape["section"], mesh.shape["ctx"] // CORES),
        mesh=mesh,
        in_specs=(spec, spec, spec, spec, P()),
        out_specs=(spec, spec, spec),
        check_vma=False,
    )
```

```python
import functools
import math

import jax
import jax.numpy as jnp
from jax import lax
from jax.experimental import pallas as pl
from jax.experimental.pallas import tpu as pltpu
from jax.sharding import PartitionSpec as P

WINDOW = 1024
KV_HEADS = 8
CORES = 2
TILE = 128

SCORE_SCALE = 168.0 ** (-0.5)
SCORE_SCALE_LOG2 = SCORE_SCALE * math.log2(math.e)
MESH = pl.DeviceIdType.MESH


def kernel(
    sections, chips,
    docs, q_in, k_in, v_in, o_in,
    dq_out, dk_out, dv_out,
    q_buf, o_buf, kv_buf, kt_buf, bias_buf, acc_k, acc_v, term_buf, got_buf, dq_buf,
    q_send, q_recv, o_send, o_recv, kv_send, kv_recv, g_send, g_recv, dq_send, dq_recv, dq_local, relay_send, relay_recv,
):
    local_heads, chip_rows, group_width = q_buf.shape
    head_size = kt_buf.shape[0]
    rows = chip_rows // CORES
    reach = WINDOW // chip_rows
    own_start = reach * chip_rows
    width = WINDOW + TILE
    tiles = chip_rows // TILE
    sec = lax.axis_index("section")
    rank = lax.axis_index("ctx")
    chip = rank // CORES
    core = rank % CORES
    other = 1 - core
    sibling = chip * CORES + other
    sec_from = lax.rem(sec + 1, sections)
    sec_to = lax.rem(sec + sections - 1, sections)

    relayed = chips == 4 and reach >= 2

    def sends_to(away):
        sends = chip + away < chips
        return sends & (chip != 1) if relayed and away == 1 else sends

    def gets_from(away):
        gets = chip >= away
        return gets & (chip != 2) if relayed and away == 1 else gets

    barrier = pltpu.get_barrier_semaphore()

    def greet(section, ctx):
        pl.semaphore_signal(barrier, inc=1, device_id=(section, ctx), device_id_type=MESH)

    greet(sec, sibling)
    for t in range(CORES):
        greet(sec_from, chip * CORES + t)
        greet(sec_to, chip * CORES + t)
    for away in range(1, reach + 1):
        @pl.when(chip >= away)
        def _():
            for t in range(CORES):
                greet(sec, (chip - away) * CORES + t)

        @pl.when(chip + away < chips)
        def _():
            for t in range(CORES):
                greet(sec, (chip + away) * CORES + t)
    peers = jnp.int32(1 + 2 * CORES)
    for away in range(1, reach + 1):
        peers = peers + jnp.where(chip >= away, CORES, 0) + jnp.where(chip + away < chips, CORES, 0)
    pl.semaphore_wait(barrier, peers)

    def aligned(start, size):
        return pl.ds(pl.multiple_of(start, size), size)

    def rows_of(c):
        return aligned(c * rows, rows)

    def group_cols(h, t):
        return aligned((t * local_heads + h) * group_width, group_width)

    def head_cols(h, t):
        return aligned((t * local_heads + h) * head_size, head_size)

    def copy_o(h, t, from_core):
        return pltpu.make_async_remote_copy(
            src_ref=o_in.at[0, :, group_cols(h, t)],
            dst_ref=o_buf.at[h, rows_of(from_core), :],
            send_sem=o_send.at[h, t],
            recv_sem=o_recv.at[h, from_core],
            device_id=(sec_to, chip * CORES + t),
            device_id_type=MESH,
        )

    def copy_q_sibling(h, from_core):
        return pltpu.make_async_remote_copy(
            src_ref=q_in.at[0, :, group_cols(h, other)],
            dst_ref=q_buf.at[h, rows_of(from_core), :],
            send_sem=q_send.at[h],
            recv_sem=q_recv.at[h, 1],
            device_id=(sec, sibling),
            device_id_type=MESH,
        )

    def copy_q_own(h):
        return pltpu.make_async_copy(
            q_in.at[0, :, group_cols(h, core)], q_buf.at[h, rows_of(core), :], q_recv.at[h, 0]
        )

    def kv_rows(away, c):
        return aligned((reach - away) * chip_rows + c * rows, rows)

    def copy_kv(h, which, away, t, from_core):
        source = (k_in, v_in)[which]
        return pltpu.make_async_remote_copy(
            src_ref=source.at[0, :, head_cols(h, t)],
            dst_ref=kv_buf.at[h, which, kv_rows(away, from_core), :],
            send_sem=kv_send.at[h, which, away * CORES + t],
            recv_sem=kv_recv.at[h, which, away * CORES + from_core],
            device_id=(sec, (chip + away) * CORES + t),
            device_id_type=MESH,
        )

    def copy_kv_own(h, which):
        source = (k_in, v_in)[which]
        return pltpu.make_async_copy(
            source.at[0, :, head_cols(h, core)],
            kv_buf.at[h, which, kv_rows(0, core), :],
            kv_recv.at[h, which, core],
        )

    def copy_relay(h):
        return pltpu.make_async_remote_copy(
            src_ref=kv_buf.at[h, :, pl.ds((reach - 2) * chip_rows, chip_rows), :],
            dst_ref=kv_buf.at[h, :, pl.ds((reach - 1) * chip_rows, chip_rows), :],
            send_sem=relay_send.at[h],
            recv_sem=relay_recv.at[h],
            device_id=(sec, (chip - 1) * CORES + core),
            device_id_type=MESH,
        )

    def copy_term(h, away, t):
        return pltpu.make_async_remote_copy(
            src_ref=term_buf.at[h, :, kv_rows(away, t), :],
            dst_ref=got_buf.at[away, core * local_heads + h],
            send_sem=g_send.at[h, away * CORES + t],
            recv_sem=g_recv.at[away, core * local_heads + h],
            device_id=(sec, (chip - away) * CORES + t),
            device_id_type=MESH,
        )

    def wait_term(g, away):
        pltpu.make_async_remote_copy(
            src_ref=term_buf.at[0, :, pl.ds(0, rows), :],
            dst_ref=got_buf.at[away, g],
            send_sem=g_send.at[0, 0],
            recv_sem=g_recv.at[away, g],
            device_id=(sec, sibling),
            device_id_type=MESH,
        ).wait_recv()

    def copy_term_own(h):
        return pltpu.make_async_copy(
            term_buf.at[h, :, kv_rows(0, core), :],
            got_buf.at[0, core * local_heads + h],
            g_recv.at[0, core * local_heads + h],
        )

    def copy_dq_sibling(h, for_core):
        return pltpu.make_async_remote_copy(
            src_ref=dq_buf.at[h, rows_of(for_core), :],
            dst_ref=dq_out.at[0, :, group_cols(h, 1 - for_core)],
            send_sem=dq_send.at[h],
            recv_sem=dq_recv.at[h],
            device_id=(sec, sibling),
            device_id_type=MESH,
        )

    def copy_dq_own(h):
        return pltpu.make_async_copy(
            dq_buf.at[h, rows_of(core), :], dq_out.at[0, :, group_cols(h, core)], dq_local.at[h]
        )

    @pl.loop(0, local_heads)
    def _(h):
        for t in range(CORES):
            copy_o(h, t, core).start()
        for which in range(2):
            for away in range(1, reach + 1):
                @pl.when(sends_to(away))
                def _():
                    for t in range(CORES):
                        copy_kv(h, which, away, t, core).start()
        copy_q_sibling(h, core).start()
        copy_q_own(h).start()
        for which in range(2):
            copy_kv(h, which, 0, other, core).start()
            copy_kv_own(h, which).start()

    for away in range(1, reach + 1):
        @pl.when(chip < away)
        def _():
            kv_buf[:, :, pl.ds((reach - away) * chip_rows, chip_rows), :] = jnp.zeros(
                (local_heads, 2, chip_rows, head_size), kv_buf.dtype
            )

        @pl.when(chip + away >= chips)
        def _():
            got_buf[away] = jnp.zeros(got_buf.shape[1:], got_buf.dtype)

    for tile in range(tiles):
        query_pos = chip * chip_rows + tile * TILE + lax.broadcasted_iota(jnp.int32, (1, TILE), 1)
        lowest = query_pos - (WINDOW - 1)
        end = jnp.int32(0)
        lowest = jnp.maximum(lowest, 0)
        for d in range(docs.shape[0]):
            end = end + docs[d]
            lowest = jnp.maximum(lowest, jnp.where(query_pos >= end, end, 0))
        key_pos = (
            chip * chip_rows - WINDOW + tile * TILE
            + lax.broadcasted_iota(jnp.int32, (width, TILE), 0)
        )
        bias_buf[tile] = jnp.where(
            (key_pos <= query_pos) & (key_pos >= lowest), 0.0, -jnp.inf
        ).astype(jnp.float32)

    def two_heads(block):
        return jnp.concatenate([block[:, :head_size], block[:, head_size:]], axis=0)

    @pl.loop(0, local_heads)
    def _(h):
        for away in range(reach, 0, -1):
            @pl.when(gets_from(away))
            def _():
                for which in range(2):
                    for c in range(CORES):
                        copy_kv(h, which, away, c, c).wait_recv()

            if relayed and away == 2:
                @pl.when(chip == 3)
                def _():
                    copy_relay(h).start()

        copy_q_own(h).wait()
        copy_q_sibling(h, other).wait_recv()
        for which in range(2):
            copy_kv_own(h, which).wait()
            copy_kv(h, which, 0, other, other).wait_recv()
        for c in range(CORES):
            copy_o(h, c, c).wait_recv()
        if relayed:
            @pl.when(chip == 2)
            def _():
                copy_relay(h).wait_recv()

        kt_buf[...] = kv_buf[h, 0].T
        acc_k[...] = jnp.zeros_like(acc_k)
        acc_v[...] = jnp.zeros_like(acc_v)

        @pl.loop(0, tiles, unroll=2)
        def _(tile):
            span = pl.ds(pl.multiple_of(tile * TILE, TILE), width)
            here = aligned(tile * TILE, TILE)
            keys = kv_buf[h, 0, span, :]
            values = kv_buf[h, 1, span, :]
            queries = two_heads(q_buf[h, here, :])
            grads = two_heads(o_buf[h, here, :])
            bias = bias_buf[tile]
            nt = (((1,), (1,)), ((), ()))
            scores = lax.dot_general(keys, queries, nt, preferred_element_type=jnp.float32)
            scores = scores * SCORE_SCALE_LOG2 + jnp.concatenate([bias, bias], axis=1)
            highest = jnp.max(scores, axis=0, keepdims=True)
            raised = jnp.exp2(scores - highest)
            weights = raised * (1.0 / jnp.sum(raised, axis=0, keepdims=True))
            weight_grad = lax.dot_general(values, grads, nt, preferred_element_type=jnp.float32)
            row_dot = jnp.sum(weights * weight_grad, axis=0, keepdims=True)
            score_grad = (weights * (weight_grad - row_dot)).astype(jnp.bfloat16)
            weight_half = weights.astype(jnp.bfloat16)
            acc_v[span, :] += jnp.dot(weight_half, grads, preferred_element_type=jnp.float32)
            acc_k[span, :] += jnp.dot(score_grad, queries, preferred_element_type=jnp.float32)
            back = jnp.dot(kt_buf[:, span], score_grad, preferred_element_type=jnp.float32)
            back = (back * SCORE_SCALE).T.astype(jnp.bfloat16)
            dq_buf[h, here, :] = jnp.concatenate([back[:TILE], back[TILE:]], axis=1)

        term_buf[h, 0] = (acc_k[...] * SCORE_SCALE).astype(jnp.bfloat16)
        term_buf[h, 1] = acc_v[...].astype(jnp.bfloat16)
        for away in range(1, reach + 1):
            @pl.when(chip >= away)
            def _():
                for t in range(CORES):
                    copy_term(h, away, t).start()
        copy_term(h, 0, other).start()
        copy_term_own(h).start()
        copy_dq_sibling(h, other).start()
        copy_dq_own(h).start()

    @pl.loop(0, local_heads)
    def _(h):
        copy_term_own(h).wait()
        wait_term(other * local_heads + h, 0)
        for away in range(1, reach + 1):
            @pl.when(chip + away < chips)
            def _():
                for t in range(CORES):
                    wait_term(t * local_heads + h, away)
        for t in range(CORES):
            g = t * local_heads + h
            total = got_buf[0, g].astype(jnp.float32)
            for away in range(1, reach + 1):
                total = total + got_buf[away, g].astype(jnp.float32)
            dk_out[0, :, head_cols(h, t)] = total[0].astype(jnp.bfloat16)
            dv_out[0, :, head_cols(h, t)] = total[1].astype(jnp.bfloat16)

    @pl.loop(0, local_heads)
    def _(h):
        copy_dq_own(h).wait()
        copy_dq_sibling(h, core).wait_recv()
        copy_dq_sibling(h, other).wait_send()
        copy_q_sibling(h, core).wait_send()
        for t in range(CORES):
            copy_o(h, t, core).wait_send()
        for which in range(2):
            copy_kv(h, which, 0, other, core).wait_send()
        copy_term(h, 0, other).wait_send()
        if relayed:
            @pl.when(chip == 3)
            def _():
                copy_relay(h).wait_send()

        for away in range(1, reach + 1):
            @pl.when(sends_to(away))
            def _():
                for which in range(2):
                    for t in range(CORES):
                        copy_kv(h, which, away, t, core).wait_send()

            @pl.when(chip >= away)
            def _():
                for t in range(CORES):
                    copy_term(h, away, t).wait_send()


def local(sections, chips, query_rows, key_rows, value_rows, finished_grad, doc_lengths):
    rows = query_rows.shape[1]
    kv_width = key_rows.shape[2]
    head_size = kv_width // KV_HEADS
    group_width = query_rows.shape[2] // KV_HEADS
    local_heads = KV_HEADS // CORES
    chip_rows = CORES * rows
    reach = WINDOW // chip_rows
    span = WINDOW + chip_rows
    half = jnp.bfloat16
    dma = pltpu.SemaphoreType.DMA
    anywhere = pl.BlockSpec(memory_space=pl.ANY)
    in_vmem = pl.BlockSpec(memory_space=pltpu.VMEM)
    pairs = 2 * (KV_HEADS // 2) * chip_rows * (WINDOW + TILE)
    return pl.pallas_call(
        functools.partial(kernel, sections, chips),
        out_shape=(
            jax.ShapeDtypeStruct(query_rows.shape, half),
            jax.ShapeDtypeStruct(key_rows.shape, half),
            jax.ShapeDtypeStruct(value_rows.shape, half),
        ),
        in_specs=[pl.BlockSpec(memory_space=pltpu.SMEM)] + [anywhere] * 4,
        out_specs=(anywhere, in_vmem, in_vmem),
        scratch_shapes=[
            pltpu.VMEM((local_heads, chip_rows, group_width), half),
            pltpu.VMEM((local_heads, chip_rows, group_width), half),
            pltpu.VMEM((local_heads, 2, span, head_size), half),
            pltpu.VMEM((head_size, span), half),
            pltpu.VMEM((chip_rows // TILE, WINDOW + TILE, TILE), jnp.float32),
            pltpu.VMEM((span, head_size), jnp.float32),
            pltpu.VMEM((span, head_size), jnp.float32),
            pltpu.VMEM((local_heads, 2, span, head_size), half),
            pltpu.VMEM((reach + 1, KV_HEADS, 2, rows, head_size), half),
            pltpu.VMEM((local_heads, chip_rows, group_width), half),
            dma((local_heads,)),
            dma((local_heads, 2)),
            dma((local_heads, CORES)),
            dma((local_heads, CORES)),
            dma((local_heads, 2, (reach + 1) * CORES)),
            dma((local_heads, 2, (reach + 1) * CORES)),
            dma((local_heads, (reach + 1) * CORES)),
            dma((reach + 1, KV_HEADS)),
            dma((local_heads,)),
            dma((local_heads,)),
            dma((local_heads,)),
            dma((local_heads,)),
            dma((local_heads,)),
        ],
        compiler_params=pltpu.CompilerParams(
            collective_id=0, has_side_effects=True, vmem_limit_bytes=63 * 1024 * 1024
        ),
        cost_estimate=pl.CostEstimate(
            flops=10 * pairs * head_size, bytes_accessed=8 * 1024 * 1024, transcendentals=pairs
        ),
    )(doc_lengths, query_rows, key_rows, value_rows, finished_grad)


def solution(mesh):
    spec = P("section", "ctx", None)
    return jax.shard_map(
        functools.partial(local, mesh.shape["section"], mesh.shape["ctx"] // CORES),
        mesh=mesh,
        in_specs=(spec, spec, spec, spec, P()),
        out_specs=(spec, spec, spec),
        check_vma=False,
    )
```

```python
import functools
import math

import jax
import jax.numpy as jnp
from jax import lax
from jax.experimental import pallas as pl
from jax.experimental.pallas import tpu as pltpu
from jax.sharding import PartitionSpec as P

WINDOW = 1024
KV_HEADS = 8
CORES = 2
TILE = 128

SCORE_SCALE = 168.0 ** (-0.5)
SCORE_SCALE_LOG2 = SCORE_SCALE * math.log2(math.e)
MESH = pl.DeviceIdType.MESH


def kernel(
    sections, chips,
    docs, q_in, k_in, v_in, o_in,
    dq_out, dk_out, dv_out,
    q_buf, o_buf, kv_buf, kt_buf, bias_buf, acc_k, acc_v, term_buf, got_buf, dq_buf,
    q_send, q_recv, o_send, o_recv, kv_send, kv_recv, g_send, g_recv, dq_send, dq_recv, dq_local, relay_send, relay_recv,
):
    local_heads, chip_rows, group_width = q_buf.shape
    head_size = kt_buf.shape[0]
    rows = chip_rows // CORES
    reach = WINDOW // chip_rows
    own_start = reach * chip_rows
    width = WINDOW + TILE
    tiles = chip_rows // TILE
    sec = lax.axis_index("section")
    rank = lax.axis_index("ctx")
    chip = rank // CORES
    core = rank % CORES
    other = 1 - core
    sibling = chip * CORES + other
    sec_from = lax.rem(sec + 1, sections)
    sec_to = lax.rem(sec + sections - 1, sections)

    relayed = False

    def sends_to(away):
        sends = chip + away < chips
        return sends & (chip != 1) if relayed and away == 1 else sends

    def gets_from(away):
        gets = chip >= away
        return gets & (chip != 2) if relayed and away == 1 else gets

    barrier = pltpu.get_barrier_semaphore()

    def greet(section, ctx):
        pl.semaphore_signal(barrier, inc=1, device_id=(section, ctx), device_id_type=MESH)

    greet(sec, sibling)
    for t in range(CORES):
        greet(sec_from, chip * CORES + t)
        greet(sec_to, chip * CORES + t)
    for away in range(1, reach + 1):
        @pl.when(chip >= away)
        def _():
            for t in range(CORES):
                greet(sec, (chip - away) * CORES + t)

        @pl.when(chip + away < chips)
        def _():
            for t in range(CORES):
                greet(sec, (chip + away) * CORES + t)
    peers = jnp.int32(1 + 2 * CORES)
    for away in range(1, reach + 1):
        peers = peers + jnp.where(chip >= away, CORES, 0) + jnp.where(chip + away < chips, CORES, 0)
    pl.semaphore_wait(barrier, peers)

    def aligned(start, size):
        return pl.ds(pl.multiple_of(start, size), size)

    def rows_of(c):
        return aligned(c * rows, rows)

    def group_cols(h, t):
        return aligned((t * local_heads + h) * group_width, group_width)

    def head_cols(h, t):
        return aligned((t * local_heads + h) * head_size, head_size)

    def copy_o(h, t, from_core):
        return pltpu.make_async_remote_copy(
            src_ref=o_in.at[0, :, group_cols(h, t)],
            dst_ref=o_buf.at[h, rows_of(from_core), :],
            send_sem=o_send.at[h, t],
            recv_sem=o_recv.at[h, from_core],
            device_id=(sec_to, chip * CORES + t),
            device_id_type=MESH,
        )

    def copy_q_sibling(h, from_core):
        return pltpu.make_async_remote_copy(
            src_ref=q_in.at[0, :, group_cols(h, other)],
            dst_ref=q_buf.at[h, rows_of(from_core), :],
            send_sem=q_send.at[h],
            recv_sem=q_recv.at[h, 1],
            device_id=(sec, sibling),
            device_id_type=MESH,
        )

    def copy_q_own(h):
        return pltpu.make_async_copy(
            q_in.at[0, :, group_cols(h, core)], q_buf.at[h, rows_of(core), :], q_recv.at[h, 0]
        )

    def kv_rows(away, c):
        return aligned((reach - away) * chip_rows + c * rows, rows)

    def copy_kv(h, which, away, t, from_core):
        source = (k_in, v_in)[which]
        return pltpu.make_async_remote_copy(
            src_ref=source.at[0, :, head_cols(h, t)],
            dst_ref=kv_buf.at[h, which, kv_rows(away, from_core), :],
            send_sem=kv_send.at[h, which, away * CORES + t],
            recv_sem=kv_recv.at[h, which, away * CORES + from_core],
            device_id=(sec, (chip + away) * CORES + t),
            device_id_type=MESH,
        )

    def copy_kv_own(h, which):
        source = (k_in, v_in)[which]
        return pltpu.make_async_copy(
            source.at[0, :, head_cols(h, core)],
            kv_buf.at[h, which, kv_rows(0, core), :],
            kv_recv.at[h, which, core],
        )

    def copy_relay(h):
        return pltpu.make_async_remote_copy(
            src_ref=kv_buf.at[h, :, pl.ds((reach - 2) * chip_rows, chip_rows), :],
            dst_ref=kv_buf.at[h, :, pl.ds((reach - 1) * chip_rows, chip_rows), :],
            send_sem=relay_send.at[h],
            recv_sem=relay_recv.at[h],
            device_id=(sec, (chip - 1) * CORES + core),
            device_id_type=MESH,
        )

    def copy_term(h, away, t):
        return pltpu.make_async_remote_copy(
            src_ref=term_buf.at[h, :, kv_rows(away, t), :],
            dst_ref=got_buf.at[away, core * local_heads + h],
            send_sem=g_send.at[h, away * CORES + t],
            recv_sem=g_recv.at[away, core * local_heads + h],
            device_id=(sec, (chip - away) * CORES + t),
            device_id_type=MESH,
        )

    def wait_term(g, away):
        pltpu.make_async_remote_copy(
            src_ref=term_buf.at[0, :, pl.ds(0, rows), :],
            dst_ref=got_buf.at[away, g],
            send_sem=g_send.at[0, 0],
            recv_sem=g_recv.at[away, g],
            device_id=(sec, sibling),
            device_id_type=MESH,
        ).wait_recv()

    def copy_term_own(h):
        return pltpu.make_async_copy(
            term_buf.at[h, :, kv_rows(0, core), :],
            got_buf.at[0, core * local_heads + h],
            g_recv.at[0, core * local_heads + h],
        )

    def copy_dq_sibling(h, for_core):
        return pltpu.make_async_remote_copy(
            src_ref=dq_buf.at[h, rows_of(for_core), :],
            dst_ref=dq_out.at[0, :, group_cols(h, 1 - for_core)],
            send_sem=dq_send.at[h],
            recv_sem=dq_recv.at[h],
            device_id=(sec, sibling),
            device_id_type=MESH,
        )

    def copy_dq_own(h):
        return pltpu.make_async_copy(
            dq_buf.at[h, rows_of(core), :], dq_out.at[0, :, group_cols(h, core)], dq_local.at[h]
        )

    @pl.loop(0, local_heads)
    def _(h):
        for t in range(CORES):
            copy_o(h, t, core).start()
        for which in range(2):
            for away in range(1, reach + 1):
                @pl.when(sends_to(away))
                def _():
                    for t in range(CORES):
                        copy_kv(h, which, away, t, core).start()
        copy_q_sibling(h, core).start()
        copy_q_own(h).start()
        for which in range(2):
            copy_kv(h, which, 0, other, core).start()
            copy_kv_own(h, which).start()

    for away in range(1, reach + 1):
        @pl.when(chip < away)
        def _():
            kv_buf[:, :, pl.ds((reach - away) * chip_rows, chip_rows), :] = jnp.zeros(
                (local_heads, 2, chip_rows, head_size), kv_buf.dtype
            )

        @pl.when(chip + away >= chips)
        def _():
            got_buf[away] = jnp.zeros(got_buf.shape[1:], got_buf.dtype)

    for tile in range(tiles):
        query_pos = chip * chip_rows + tile * TILE + lax.broadcasted_iota(jnp.int32, (1, TILE), 1)
        lowest = query_pos - (WINDOW - 1)
        end = jnp.int32(0)
        lowest = jnp.maximum(lowest, 0)
        for d in range(docs.shape[0]):
            end = end + docs[d]
            lowest = jnp.maximum(lowest, jnp.where(query_pos >= end, end, 0))
        key_pos = (
            chip * chip_rows - WINDOW + tile * TILE
            + lax.broadcasted_iota(jnp.int32, (width, TILE), 0)
        )
        bias_buf[tile] = jnp.where(
            (key_pos <= query_pos) & (key_pos >= lowest), 0.0, -jnp.inf
        ).astype(jnp.float32)

    def two_heads(block):
        return jnp.concatenate([block[:, :head_size], block[:, head_size:]], axis=0)

    @pl.loop(0, local_heads)
    def _(h):
        for away in range(reach, 0, -1):
            @pl.when(gets_from(away))
            def _():
                for which in range(2):
                    for c in range(CORES):
                        copy_kv(h, which, away, c, c).wait_recv()

            if relayed and away == 2:
                @pl.when(chip == 3)
                def _():
                    copy_relay(h).start()

        copy_q_own(h).wait()
        copy_q_sibling(h, other).wait_recv()
        for which in range(2):
            copy_kv_own(h, which).wait()
            copy_kv(h, which, 0, other, other).wait_recv()
        for c in range(CORES):
            copy_o(h, c, c).wait_recv()
        if relayed:
            @pl.when(chip == 2)
            def _():
                copy_relay(h).wait_recv()

        kt_buf[...] = kv_buf[h, 0].T
        acc_k[...] = jnp.zeros_like(acc_k)
        acc_v[...] = jnp.zeros_like(acc_v)

        @pl.loop(0, tiles, unroll=2)
        def _(tile):
            span = pl.ds(pl.multiple_of(tile * TILE, TILE), width)
            here = aligned(tile * TILE, TILE)
            keys = kv_buf[h, 0, span, :]
            values = kv_buf[h, 1, span, :]
            queries = two_heads(q_buf[h, here, :])
            grads = two_heads(o_buf[h, here, :])
            bias = bias_buf[tile]
            nt = (((1,), (1,)), ((), ()))
            scores = lax.dot_general(keys, queries, nt, preferred_element_type=jnp.float32)
            scores = scores * SCORE_SCALE_LOG2 + jnp.concatenate([bias, bias], axis=1)
            highest = jnp.max(scores, axis=0, keepdims=True)
            raised = jnp.exp2(scores - highest)
            weights = raised * (1.0 / jnp.sum(raised, axis=0, keepdims=True))
            weight_grad = lax.dot_general(values, grads, nt, preferred_element_type=jnp.float32)
            row_dot = jnp.sum(weights * weight_grad, axis=0, keepdims=True)
            score_grad = (weights * (weight_grad - row_dot)).astype(jnp.bfloat16)
            weight_half = weights.astype(jnp.bfloat16)
            acc_v[span, :] += jnp.dot(weight_half, grads, preferred_element_type=jnp.float32)
            acc_k[span, :] += jnp.dot(score_grad, queries, preferred_element_type=jnp.float32)
            back = jnp.dot(kt_buf[:, span], score_grad, preferred_element_type=jnp.float32)
            back = (back * SCORE_SCALE).T.astype(jnp.bfloat16)
            dq_buf[h, here, :] = jnp.concatenate([back[:TILE], back[TILE:]], axis=1)

        term_buf[h, 0] = (acc_k[...] * SCORE_SCALE).astype(jnp.bfloat16)
        term_buf[h, 1] = acc_v[...].astype(jnp.bfloat16)
        for away in range(1, reach + 1):
            @pl.when(chip >= away)
            def _():
                for t in range(CORES):
                    copy_term(h, away, t).start()
        copy_term(h, 0, other).start()
        copy_term_own(h).start()
        copy_dq_sibling(h, other).start()
        copy_dq_own(h).start()

    @pl.loop(0, local_heads)
    def _(h):
        copy_term_own(h).wait()
        wait_term(other * local_heads + h, 0)
        for away in range(1, reach + 1):
            @pl.when(chip + away < chips)
            def _():
                for t in range(CORES):
                    wait_term(t * local_heads + h, away)
        for t in range(CORES):
            g = t * local_heads + h
            total = got_buf[0, g].astype(jnp.float32)
            for away in range(1, reach + 1):
                total = total + got_buf[away, g].astype(jnp.float32)
            dk_out[0, :, head_cols(h, t)] = total[0].astype(jnp.bfloat16)
            dv_out[0, :, head_cols(h, t)] = total[1].astype(jnp.bfloat16)

    @pl.loop(0, local_heads)
    def _(h):
        copy_dq_own(h).wait()
        copy_dq_sibling(h, core).wait_recv()
        copy_dq_sibling(h, other).wait_send()
        copy_q_sibling(h, core).wait_send()
        for t in range(CORES):
            copy_o(h, t, core).wait_send()
        for which in range(2):
            copy_kv(h, which, 0, other, core).wait_send()
        copy_term(h, 0, other).wait_send()
        if relayed:
            @pl.when(chip == 3)
            def _():
                copy_relay(h).wait_send()

        for away in range(1, reach + 1):
            @pl.when(sends_to(away))
            def _():
                for which in range(2):
                    for t in range(CORES):
                        copy_kv(h, which, away, t, core).wait_send()

            @pl.when(chip >= away)
            def _():
                for t in range(CORES):
                    copy_term(h, away, t).wait_send()


def local(sections, chips, query_rows, key_rows, value_rows, finished_grad, doc_lengths):
    rows = query_rows.shape[1]
    kv_width = key_rows.shape[2]
    head_size = kv_width // KV_HEADS
    group_width = query_rows.shape[2] // KV_HEADS
    local_heads = KV_HEADS // CORES
    chip_rows = CORES * rows
    reach = WINDOW // chip_rows
    span = WINDOW + chip_rows
    half = jnp.bfloat16
    dma = pltpu.SemaphoreType.DMA
    anywhere = pl.BlockSpec(memory_space=pl.ANY)
    in_vmem = pl.BlockSpec(memory_space=pltpu.VMEM)
    pairs = 2 * (KV_HEADS // 2) * chip_rows * (WINDOW + TILE)
    return pl.pallas_call(
        functools.partial(kernel, sections, chips),
        out_shape=(
            jax.ShapeDtypeStruct(query_rows.shape, half),
            jax.ShapeDtypeStruct(key_rows.shape, half),
            jax.ShapeDtypeStruct(value_rows.shape, half),
        ),
        in_specs=[pl.BlockSpec(memory_space=pltpu.SMEM)] + [anywhere] * 4,
        out_specs=(anywhere, in_vmem, in_vmem),
        scratch_shapes=[
            pltpu.VMEM((local_heads, chip_rows, group_width), half),
            pltpu.VMEM((local_heads, chip_rows, group_width), half),
            pltpu.VMEM((local_heads, 2, span, head_size), half),
            pltpu.VMEM((head_size, span), half),
            pltpu.VMEM((chip_rows // TILE, WINDOW + TILE, TILE), jnp.float32),
            pltpu.VMEM((span, head_size), jnp.float32),
            pltpu.VMEM((span, head_size), jnp.float32),
            pltpu.VMEM((local_heads, 2, span, head_size), half),
            pltpu.VMEM((reach + 1, KV_HEADS, 2, rows, head_size), half),
            pltpu.VMEM((local_heads, chip_rows, group_width), half),
            dma((local_heads,)),
            dma((local_heads, 2)),
            dma((local_heads, CORES)),
            dma((local_heads, CORES)),
            dma((local_heads, 2, (reach + 1) * CORES)),
            dma((local_heads, 2, (reach + 1) * CORES)),
            dma((local_heads, (reach + 1) * CORES)),
            dma((reach + 1, KV_HEADS)),
            dma((local_heads,)),
            dma((local_heads,)),
            dma((local_heads,)),
            dma((local_heads,)),
            dma((local_heads,)),
        ],
        compiler_params=pltpu.CompilerParams(
            collective_id=0, has_side_effects=True, vmem_limit_bytes=63 * 1024 * 1024
        ),
        cost_estimate=pl.CostEstimate(
            flops=10 * pairs * head_size, bytes_accessed=8 * 1024 * 1024, transcendentals=pairs
        ),
    )(doc_lengths, query_rows, key_rows, value_rows, finished_grad)


def solution(mesh):
    spec = P("section", "ctx", None)
    return jax.shard_map(
        functools.partial(local, mesh.shape["section"], mesh.shape["ctx"] // CORES),
        mesh=mesh,
        in_specs=(spec, spec, spec, spec, P()),
        out_specs=(spec, spec, spec),
        check_vma=False,
    )
```
